32 devices in a mesh: dp: 4 (over y, core), tensor: 8 (over z, x).
Axes of the slice: x: 2, y: 2, z: 4, core: 2. Of those that a mesh axis runs over, the one named last changes fastest.
Arguments:
- gradient: bfloat16 [2048, 7168], P('dp', 'tensor'), may hold values from -8000 to 8000
- block_owner: int32 [56], replicated, may hold values from 0 to 63, as said below
- tile_block: int32 [4, 56], replicated, may hold values from 0 to 55, as said below
- fast_weight: float32 [2048, 7168], P('dp', 'tensor'), may hold values from -6 to 6
- slow_flat: float32 [2048, 7168], P(('dp', 'tensor')), may hold values from -6 to 6
- left_stat: float32 [64, 512, 512], P(('dp', 'tensor')), may hold values from -6 to 6
- right_stat: float32 [64, 512, 512], P(('dp', 'tensor')), may hold values from -6 to 6
- left_basis: bfloat16 [64, 512, 512], P(('dp', 'tensor')), may hold values from -0.25 to 0.25
- right_basis: bfloat16 [64, 512, 512], P(('dp', 'tensor')), may hold values from -0.25 to 0.25
- first_moment: float32 [64, 512, 512], P(('dp', 'tensor')), may hold values from -3 to 3
- second_moment: float32 [64, 512, 512], P(('dp', 'tensor')), may hold values from 0.05 to 0.5
Outputs:
- fast_new: float32 [2048, 7168], P('dp', 'tensor')
- slow_new: float32 [2048, 7168], P(('dp', 'tensor'))
- left_new: float32 [64, 512, 512], P(('dp', 'tensor'))
- right_new: float32 [64, 512, 512], P(('dp', 'tensor'))
- moment_new: float32 [64, 512, 512], P(('dp', 'tensor'))
- second_new: float32 [64, 512, 512], P(('dp', 'tensor'))
The draws below stay inside these ranges and needn't reach their ends.
Inputs may be any that keep to these rules, and one draw needn't show every extreme that they name: `tile_block`: entry [r, g] is the number of the block that tile g of block row r (columns g * 128 to g * 128 + 127) belongs to, one of r * (14) to r * 14 + 7168 // 512 - 1. Each such block has 4 tiles, which lie in the columns of different tensor indices. In each row the tensor indices fall into groups of 4, and every block takes one tile from each member of one group. `block_owner`: entry b is the slot d * 2 + k of block b's owner, where d = (dp index) * (number of tensor indices) + (tensor index) and k is 0 or 1; the owner's dp index is the block's row. No slot is named twice, every device owns one or two blocks, and a device's two blocks come from different groups.
All inputs are finite; a program needn't handle non-finite values.
Results may differ from the reference program's by a relative error of at most 0.00095.
Values may be sent and summed in bfloat16 or wider, within the bound.
A program may use at most 128 MiB of HBM per device.

```python
import math
import jax
import jax.numpy as jnp
from jax import lax

B = 512
TILE = 128
SHARD_COLS = 896
SLOTS = 2
ROWS = 2048
COLS = 7168
SLOT_TOTAL = 64
N_TENSOR = 8


def draw_gradient(key, part):
    noise_key, row_key, col_key = jax.random.split(key, 3)
    noise = jnp.clip(jax.random.normal(noise_key, (ROWS, COLS), jnp.float32), -6.0, 6.0)
    trend_rows = jnp.exp(math.log(3.0) * jnp.arange(ROWS, dtype=jnp.float32) / ROWS)
    trend_cols = jnp.exp(math.log(3.0) * jnp.arange(COLS, dtype=jnp.float32) / COLS)
    row_scale = jnp.exp(jax.random.uniform(row_key, (ROWS,), jnp.float32, 0.0, math.log(2.0)))
    col_scale = jnp.exp(jax.random.uniform(col_key, (COLS,), jnp.float32, 0.0, math.log(2.0)))
    rows_part = (row_scale * trend_rows)[:, None]
    cols_part = (col_scale * trend_cols)[None, :]
    return jnp.clip(noise * rows_part * cols_part, -8000.0, 8000.0).astype(jnp.bfloat16)


def layout_tables(key):
    base_key = jax.random.fold_in(key, 11)
    row_blocks = SHARD_COLS * N_TENSOR // B
    per_block = B // TILE
    shard_tiles = SHARD_COLS // TILE
    pair_count = row_blocks - N_TENSOR
    half_count = row_blocks // 2
    row_groups = ROWS // B

    def shuffle(tile_key):
        return jax.random.permutation(tile_key, shard_tiles)

    def one_row(row_key, block_row):
        subkeys = jax.random.split(row_key, 5)
        members = jax.random.permutation(subkeys[0], N_TENSOR)
        position = jnp.argsort(members).astype(jnp.int32)
        group_of = position // per_block
        tile_keys = jax.random.split(subkeys[1], N_TENSOR)
        tile_perm = jax.vmap(shuffle)(tile_keys).astype(jnp.int32)
        local_block = group_of[:, None] * shard_tiles + tile_perm
        relabel = jax.random.permutation(subkeys[2], row_blocks).astype(jnp.int32)
        tile_numbers = block_row * row_blocks + jnp.take(relabel, local_block.reshape(-1))
        owner_perm = jax.random.permutation(subkeys[3], N_TENSOR).astype(jnp.int32)
        flip_bits = jax.random.randint(subkeys[4], (row_blocks,), 0, 2).astype(jnp.int32)
        local_ids = jnp.arange(row_blocks, dtype=jnp.int32)
        second = local_ids >= half_count
        pair_pos = jnp.where(second, local_ids - half_count, local_ids)
        paired = pair_pos < pair_count
        single = jnp.where(second, half_count - pair_count + local_ids - half_count - pair_count, local_ids - pair_count)
        owner_index = jnp.where(paired, pair_pos, pair_count + single)
        device = jnp.take(owner_perm, owner_index)
        slot_bit = jnp.where(paired, (second.astype(jnp.int32) + jnp.take(flip_bits, pair_pos)) % 2, flip_bits)
        owner_value = (block_row * N_TENSOR + device) * SLOTS + slot_bit
        inverse = jnp.argsort(relabel).astype(jnp.int32)
        owners = jnp.take(owner_value, inverse)
        return (tile_numbers, owners)
    row_keys = jax.random.split(base_key, row_groups)
    tile_numbers, owners = jax.vmap(one_row)(row_keys, jnp.arange(row_groups, dtype=jnp.int32))
    return (tile_numbers.astype(jnp.int32), owners.reshape(-1).astype(jnp.int32))


def draw_tile_block(key, part):
    return layout_tables(key)[0]


def draw_block_owner(key, part):
    return layout_tables(key)[1]


def levels(stream_key, shape, shards, low, largest):
    gain = 1.0
    for dim, parts in shards:
        heights = jax.random.uniform(jax.random.fold_in(jax.random.fold_in(stream_key, 6), dim), (parts,), jnp.float32, low / len(shards), largest / len(shards))
        gain = gain * jnp.repeat(jnp.exp(heights), shape[dim] // parts).reshape((-1,) + (1,) * (len(shape) - 1 - dim))
    return gain


def gaussian(key, dims, spread, bound, pieces=(), kind=jnp.bfloat16):
    factor_of = levels(key, dims, pieces, -0.22, 0.18) if pieces else 1.0
    drawn = jax.random.normal(key, dims, jnp.float32) * spread * factor_of
    return jnp.minimum(jnp.maximum(drawn, -bound), bound).astype(kind)


def setup_inputs(seed: int = 0) -> dict:
    seeds = jax.random.split(jax.random.key(seed), 12)
    gradient = draw_gradient(jax.random.fold_in(seeds[11], 71), 0)
    block_owner = draw_block_owner(jax.random.fold_in(seeds[11], 71), 0)
    tile_block = draw_tile_block(jax.random.fold_in(seeds[11], 71), 0)
    fast_weight = gaussian(seeds[3], (ROWS, COLS), 1.0, 6.0, ((0, 4), (1, 8)), jnp.float32)
    slow_flat = gaussian(seeds[4], (ROWS, COLS), 1.0, 6.0, ((0, 32),), jnp.float32)
    left_stat = gaussian(seeds[5], (SLOT_TOTAL, B, B), 1.0, 6.0, ((0, 32),), jnp.float32)
    right_stat = gaussian(seeds[6], (SLOT_TOTAL, B, B), 1.0, 6.0, ((0, 32),), jnp.float32)
    left_basis = gaussian(seeds[7], (SLOT_TOTAL, B, B), B ** -0.5, 0.25, ((0, 32),))
    right_basis = gaussian(seeds[8], (SLOT_TOTAL, B, B), B ** -0.5, 0.25, ((0, 32),))
    first_moment = gaussian(seeds[9], (SLOT_TOTAL, B, B), 0.5, 3.0, ((0, 32),), jnp.float32)
    second_moment = jnp.clip(jnp.exp(math.log(0.5) - 2.3025851 * jax.random.uniform(seeds[10], (SLOT_TOTAL, B, B), jnp.float32) ** levels(seeds[10], (SLOT_TOTAL, B, B), ((0, 32),), -0.2, 0.2)), 0.05, 0.5)
    return dict(gradient=gradient, block_owner=block_owner, tile_block=tile_block, fast_weight=fast_weight, slow_flat=slow_flat, left_stat=left_stat, right_stat=right_stat, left_basis=left_basis, right_basis=right_basis, first_moment=first_moment, second_moment=second_moment)


BETA_STAT = 0.95
BETA_ONE = 0.9
BETA_TWO = 0.95
ADAM_EPS = 1e-08
STEP_RATE = 0.1
PULL_RATE = 0.5
CLIP_RMS = 0.5
HIGHEST = lax.Precision.HIGHEST

def soap_block(grad_block, factor, left_stat, right_stat, left_basis, right_basis, first_moment, second_moment):
    gram_left = jnp.dot(grad_block, grad_block.T, preferred_element_type=jnp.float32)
    gram_right = jnp.dot(grad_block.T, grad_block, preferred_element_type=jnp.float32)
    squared = factor * factor
    left_next = BETA_STAT * left_stat + (1.0 - BETA_STAT) * squared * gram_left
    right_next = BETA_STAT * right_stat + (1.0 - BETA_STAT) * squared * gram_right
    left_wide = left_basis.astype(jnp.float32)
    right_wide = right_basis.astype(jnp.float32)
    half_rotated = jnp.dot(left_basis.T, grad_block, preferred_element_type=jnp.float32)
    rotated = factor * jnp.dot(half_rotated, right_wide, precision=HIGHEST)
    moment_next = BETA_ONE * first_moment + (1.0 - BETA_ONE) * factor * grad_block.astype(jnp.float32)
    second_next = BETA_TWO * second_moment + (1.0 - BETA_TWO) * rotated * rotated
    moment_turned = jnp.dot(jnp.dot(left_wide.T, moment_next, precision=HIGHEST), right_wide, precision=HIGHEST)
    direction = moment_turned / (jnp.sqrt(second_next) + ADAM_EPS)
    update = jnp.dot(jnp.dot(left_wide, direction, precision=HIGHEST), right_wide.T, precision=HIGHEST)
    return (left_next, right_next, moment_next, second_next, update.astype(jnp.bfloat16))

def reference(gradient, block_owner, tile_block, fast_weight, slow_flat, left_stat, right_stat, left_basis, right_basis, first_moment, second_moment):
    row_count, col_count = gradient.shape
    block_size = left_stat.shape[1]
    row_groups = row_count // block_size
    tile_count = tile_block.shape[1]
    tile_width = col_count // tile_count
    per_block = block_size // tile_width
    row_blocks = col_count // block_size
    wide_grad = gradient.astype(jnp.float32)
    factor = CLIP_RMS / jnp.sqrt(jnp.mean(wide_grad * wide_grad) + 1e-06)
    tile_ids = jnp.arange(tile_count, dtype=jnp.int32)
    tile_order = jnp.argsort(tile_block.astype(jnp.int32) * tile_count + tile_ids[None, :], axis=1).astype(jnp.int32)
    block_tiles = tile_order.reshape(row_groups * row_blocks, per_block)
    tiled_grad = gradient.reshape(row_groups, block_size, tile_count, tile_width)

    def one_block(block_index):
        block_row = block_index // row_blocks
        row_tiles = lax.dynamic_index_in_dim(tiled_grad, block_row, 0, keepdims=False)
        picked = lax.dynamic_index_in_dim(block_tiles, block_index, 0, keepdims=False)
        grad_block = jnp.take(row_tiles, picked, axis=1).reshape(block_size, block_size)
        owner_slot = block_owner[block_index]

        def choose(states):
            return lax.dynamic_index_in_dim(states, owner_slot, 0, keepdims=False)
        return soap_block(grad_block, factor, choose(left_stat), choose(right_stat), choose(left_basis), choose(right_basis), choose(first_moment), choose(second_moment))
    results = lax.map(one_block, jnp.arange(block_owner.shape[0], dtype=jnp.int32))
    left_new = left_stat.at[block_owner].set(results[0])
    right_new = right_stat.at[block_owner].set(results[1])
    moment_new = first_moment.at[block_owner].set(results[2])
    second_new = second_moment.at[block_owner].set(results[3])
    update = results[4].reshape(row_groups, row_blocks, block_size, per_block, tile_width)
    update = update.transpose(0, 1, 3, 2, 4).reshape(row_groups, tile_count, block_size, tile_width)
    placed = jnp.zeros_like(update)
    placed = placed.at[jnp.arange(row_groups, dtype=jnp.int32)[:, None], tile_order].set(update)
    update = placed.transpose(0, 2, 1, 3).reshape(row_count, col_count)
    fast_new = fast_weight - STEP_RATE * update.astype(jnp.float32)
    slow_new = slow_flat + PULL_RATE * (fast_new - slow_flat)
    return (fast_new, slow_new, left_new, right_new, moment_new, second_new)
```

```python
import functools

import jax
import jax.numpy as jnp
from jax import lax
from jax.experimental import pallas as pl
from jax.experimental.pallas import tpu as pltpu
from jax.sharding import PartitionSpec as P

BETA_STAT = 0.95
BETA_ONE = 0.9
BETA_TWO = 0.95
ADAM_EPS = 1e-08
STEP_RATE = 0.1
PULL_RATE = 0.5
CLIP_RMS = 0.5
F32 = jnp.float32
BF16 = jnp.bfloat16
ANY = pl.BlockSpec(memory_space=pl.ANY)
SMEM = pl.BlockSpec(memory_space=pltpu.SMEM)


def mm(a, b):
    return jnp.dot(a, b, preferred_element_type=F32)


def mm_nt(a, b):
    return lax.dot_general(a, b, (((1,), (1,)), ((), ())), preferred_element_type=F32)


def halves(x):
    high = x.astype(BF16)
    return high, (x - high.astype(F32)).astype(BF16)


def body(
    sizes,
    owner_ref, tiles_ref, grad_hbm, fast_hbm, left_hbm, right_hbm, lbase_hbm, rbase_hbm, first_hbm, second_hbm,
    home_out, flat_out, left_out, right_out, first_out, second_out,
    gt, pack, recv, back, returned, pieces, rowsr, home, flat,
    fast_v, coded, coded_r, scale, scale_r,
    left_v, right_v, lbase, rbase, lbase_t, first_v, second_v, pre, gblk,
    part, tens_sum, dp_part, dp_sum, table,
    in_sems, grad_sems, out_sems, g_send, g_recv, f_send, f_recv, c_send, c_recv, b_send, b_recv, r_send, r_recv,
    s_send, s_recv, d_send, d_recv, own_sems,
):
    n_dp, n_t, slots, tile, shard_tiles, per_block, rows_flat, row_blocks, total = sizes
    t = lax.axis_index("tensor")
    dp = lax.axis_index("dp")

    def local(src, dst, sem):
        c = pltpu.make_async_copy(src, dst, sem)
        c.start()
        return c

    grad_in = [
        local(grad_hbm.at[:, pl.ds(i * tile, tile)], gt.at[i], grad_sems.at[i]) for i in range(shard_tiles)
    ]
    lb_in = local(lbase_hbm, lbase, in_sems.at[0])
    first_in = local(first_hbm, first_v, in_sems.at[1])
    rb_in = local(rbase_hbm, rbase, in_sems.at[2])
    second_in = local(second_hbm, second_v, in_sems.at[3])
    fast_in = local(fast_hbm, fast_v, in_sems.at[6])
    left_in = local(left_hbm, left_v, in_sems.at[4])
    right_in = local(right_hbm, right_v, in_sems.at[5])

    def to_t(d):
        return {"tensor": lax.rem(t + d, n_t)}

    def to_d(d):
        return {"dp": lax.rem(dp + d, n_dp)}

    barrier = pltpu.get_barrier_semaphore()
    for d in range(1, n_t):
        pl.semaphore_signal(barrier, inc=1, device_id=to_t(d), device_id_type=pl.DeviceIdType.MESH)
    for d in range(1, n_dp):
        pl.semaphore_signal(barrier, inc=1, device_id=to_d(d), device_id_type=pl.DeviceIdType.MESH)

    tb = [tiles_ref[dp, g] for g in range(n_t * shard_tiles)]
    my_owner = [
        lax.rem(owner_ref[tiles_ref[dp, t * shard_tiles + i]] // slots, n_t) for i in range(shard_tiles)
    ]
    send_tile = []
    for p in range(n_t):
        idx = jnp.int32(0)
        for i in range(shard_tiles):
            idx = jnp.where(my_owner[i] == p, i, idx)
        send_tile.append(idx)

    for c in grad_in:
        c.wait()

    def square(i, acc):
        wide = gt[i].astype(F32)
        return acc + jnp.sum((wide * wide).reshape(-1, 8, tile), axis=0)

    part[...] = lax.fori_loop(0, shard_tiles, square, jnp.zeros((8, tile), F32))
    for p in range(n_t):
        pack[p] = gt[send_tile[p]]
    pl.semaphore_wait(barrier, n_t + n_dp - 2)

    def remote(src, dst, ssem, rsem, to):
        return pltpu.make_async_remote_copy(
            src_ref=src, dst_ref=dst, send_sem=ssem, recv_sem=rsem, device_id=to,
            device_id_type=pl.DeviceIdType.MESH,
        )

    def peer(d):
        return lax.rem(t + d, n_t)

    def origin(d):
        return lax.rem(t + n_t - d, n_t)

    def sum_copy(d, slot):
        return remote(part, tens_sum.at[slot], s_send.at[d], s_recv.at[slot], to_t(d))

    def grad_copy(d, slot):
        return remote(pack.at[peer(d)], recv.at[slot], g_send.at[d], g_recv.at[slot], to_t(d))

    def code_copy(d, slot):
        return remote(coded.at[peer(d)], coded_r.at[slot], f_send.at[d], f_recv.at[slot], to_t(d))

    def scale_copy(d, slot):
        return remote(scale.at[peer(d)], scale_r.at[slot], c_send.at[d], c_recv.at[slot], to_t(d))

    def dp_copy(d, slot):
        return remote(dp_part, dp_sum.at[slot], d_send.at[d], d_recv.at[slot], to_d(d))

    def back_copy(d, slot):
        return remote(back.at[peer(d)], returned.at[slot], b_send.at[d], b_recv.at[slot], to_t(d))

    def rows_copy(d, k, slot):
        return remote(
            pieces.at[pl.ds(k * per_block, per_block), pl.ds(peer(d) * rows_flat, rows_flat), :],
            rowsr.at[pl.ds((slot * slots + k) * per_block, per_block)],
            r_send.at[k, d], r_recv.at[k, slot], to_t(d),
        )

    others = range(1, n_t)
    for d in others:
        sum_copy(d, t).start()
    for d in others:
        grad_copy(d, t).start()
    own_grad = local(pack.at[t], recv.at[t], own_sems.at[0])

    rank = []
    for a in range(n_t):
        count = jnp.int32(0)
        for b in range(a):
            same = tb[b * shard_tiles] == tb[a * shard_tiles]
            for i in range(1, shard_tiles):
                same = same | (tb[b * shard_tiles + i] == tb[a * shard_tiles])
            count = count + same.astype(jnp.int32)
        rank.append(count)
    present = []
    source = [jnp.int32(0)] * n_t
    for k in range(slots):
        block = jnp.int32(-1)
        slot_id = (dp * n_t + t) * slots + k
        for r in range(row_blocks):
            number = dp * row_blocks + r
            block = jnp.where(owner_ref[number] == slot_id, number, block)
        present.append(block >= 0)
        places = [jnp.int32(0)] * per_block
        for a in range(n_t):
            has = tb[a * shard_tiles] == block
            for i in range(1, shard_tiles):
                has = has | (tb[a * shard_tiles + i] == block)
            source[a] = jnp.where(has, k * per_block + rank[a], source[a])
            for j in range(per_block):
                places[j] = jnp.where(has & (rank[a] == j), a, places[j])
        for j in range(per_block):
            table[k * per_block + j] = places[j]
        table[slots * per_block + k] = (block >= 0).astype(jnp.int32)

    lb_in.wait()
    rb_in.wait()
    first_in.wait()

    def before(k, carry):
        turned = lbase[k].astype(F32).T.astype(BF16)
        lbase_t[k] = turned
        high, low = halves(first_v[k])
        high, low = halves(mm(turned, high) + mm(turned, low))
        pre[k] = BETA_ONE * (mm(high, rbase[k]) + mm(low, rbase[k]))
        return carry

    lax.fori_loop(0, slots, before, 0)

    fast_in.wait()

    def encode(p, carry):
        x = fast_v[pl.ds(pl.multiple_of(p * rows_flat, 16), rows_flat), :]
        top = jnp.maximum(jnp.max(jnp.abs(x), axis=1, keepdims=True), 1e-30)
        coded[p] = jnp.floor(x * (32767.0 / top) + 0.5).astype(jnp.int32).astype(jnp.int16)
        wide = jnp.broadcast_to(top * (1.0 / 32767.0), (rows_flat, tile))
        scale[p] = jnp.concatenate([wide] * (tile // rows_flat), axis=0).T[:8]
        return carry

    lax.fori_loop(0, n_t, encode, 0)

    for d in others:
        sum_copy(d, origin(d)).wait_recv()
    tens_sum[t] = part[...]
    dp_part[...] = jnp.sum(tens_sum[...], axis=0)
    for d in range(1, n_dp):
        dp_copy(d, dp).start()
    dp_sum[dp] = dp_part[...]
    for d in range(1, n_dp):
        dp_copy(d, lax.rem(dp + n_dp - d, n_dp)).wait_recv()
    square_sum = jnp.sum(jnp.sum(dp_sum[...], axis=0), axis=(0, 1), keepdims=True)
    factor = CLIP_RMS / jnp.sqrt(square_sum / total + 1e-06)

    for d in others:
        grad_copy(d, t).wait_send()
    for d in others:
        code_copy(d, t).start()
        scale_copy(d, t).start()
    coded_r[t] = coded[t]
    scale_r[t] = scale[t]
    own_grad.wait()
    for d in others:
        grad_copy(d, origin(d)).wait_recv()
    second_in.wait()

    def main(k, carry):
        for j in range(per_block):
            gblk[k, :, j * tile : (j + 1) * tile] = recv[table[k * per_block + j]]
        there = table[slots * per_block + k] > 0
        g = gblk[k]
        high, low = halves(mm(lbase_t[k], g))
        rotated = factor * (mm(high, rbase[k]) + mm(low, rbase[k]))
        fresh = BETA_TWO * second_v[k] + (1.0 - BETA_TWO) * rotated * rotated
        second_v[k] = jnp.where(there, fresh, second_v[k])
        direction = (pre[k] + (1.0 - BETA_ONE) * rotated) / (jnp.sqrt(fresh) + ADAM_EPS)
        high, low = halves(direction)
        high, low = halves(mm(lbase[k], high) + mm(lbase[k], low))
        update = (mm_nt(high, rbase[k]) + mm_nt(low, rbase[k])).astype(BF16)
        for j in range(per_block):
            pieces[k * per_block + j] = update[:, j * tile : (j + 1) * tile]
        return carry

    lax.fori_loop(0, slots, main, 0)
    for p in range(n_t):
        back[p] = pieces[source[p]]
    for d in others:
        back_copy(d, t).start()
    for k in range(slots):
        for d in others:
            rows_copy(d, k, t).start()
    own_back = local(back.at[t], returned.at[t], own_sems.at[2])
    own_rows = [
        local(
            pieces.at[pl.ds(k * per_block, per_block), pl.ds(t * rows_flat, rows_flat), :],
            rowsr.at[pl.ds((t * slots + k) * per_block, per_block)],
            own_sems.at[3 + k],
        )
        for k in range(slots)
    ]

    left_in.wait()
    right_in.wait()
    squared = (1.0 - BETA_STAT) * (factor * factor)

    def after(k, carry):
        there = table[slots * per_block + k] > 0
        g = gblk[k]
        wide = g.astype(F32)
        turned = wide.T.astype(BF16)
        left_v[k] = jnp.where(there, BETA_STAT * left_v[k] + squared * mm_nt(g, g), left_v[k])
        right_v[k] = jnp.where(there, BETA_STAT * right_v[k] + squared * mm(turned, g), right_v[k])
        first_v[k] = jnp.where(
            there, BETA_ONE * first_v[k] + ((1.0 - BETA_ONE) * factor) * wide, first_v[k]
        )
        return carry

    second_done = local(second_v, second_out, out_sems.at[0])
    lax.fori_loop(0, slots, after, 0)
    done = [
        second_done,
        local(left_v, left_out, out_sems.at[1]),
        local(right_v, right_out, out_sems.at[2]),
        local(first_v, first_out, out_sems.at[3]),
    ]

    for d in others:
        code_copy(d, origin(d)).wait_recv()
        scale_copy(d, origin(d)).wait_recv()
    for a in range(n_t):
        step = jnp.broadcast_to(scale_r[a, 0:1, :], (tile, tile)).T[:rows_flat]
        for i in range(shard_tiles):
            g = a * shard_tiles + i
            words = coded_r[a, :, i * tile : (i + 1) * tile].astype(jnp.int32)
            flat[:, g * tile : (g + 1) * tile] = words.astype(F32) * step
    own_back.wait()
    for d in others:
        back_copy(d, origin(d)).wait_recv()
    for i in range(shard_tiles):
        home[:, i * tile : (i + 1) * tile] = returned[my_owner[i]]
    done.append(local(home, home_out, out_sems.at[4]))
    for c in own_rows:
        c.wait()
    for k in range(slots):
        for d in others:
            rows_copy(d, k, origin(d)).wait_recv()
    for a in range(n_t):
        for i in range(shard_tiles):
            g = a * shard_tiles + i
            place = lax.rem(owner_ref[tb[g]], n_t * slots) * per_block + rank[a]
            at = slice(g * tile, (g + 1) * tile)
            flat[:, at] = flat[:, at] - STEP_RATE * rowsr[place].astype(F32)
    done.append(local(flat, flat_out, out_sems.at[5]))
    for d in others:
        sum_copy(d, t).wait_send()
        code_copy(d, t).wait_send()
        scale_copy(d, t).wait_send()
        back_copy(d, t).wait_send()
        for k in range(slots):
            rows_copy(d, k, t).wait_send()
    for d in range(1, n_dp):
        dp_copy(d, dp).wait_send()
    for c in done:
        c.wait()


def on_device(
    gradient, block_owner, tile_block, fast_weight, slow_flat,
    left_stat, right_stat, left_basis, right_basis, first_moment, second_moment,
):
    block = left_stat.shape[1]
    slots = left_stat.shape[0]
    rows, shard_cols = gradient.shape
    n_t = lax.axis_size("tensor")
    n_dp = lax.axis_size("dp")
    tile_count = tile_block.shape[1]
    cols = shard_cols * n_t
    tile = cols // tile_count
    shard_tiles = shard_cols // tile
    per_block = block // tile
    rows_flat = block // n_t
    row_blocks = block_owner.shape[0] // n_dp
    sizes = (n_dp, n_t, slots, tile, shard_tiles, per_block, rows_flat, row_blocks, rows * cols * n_dp)
    vm = pltpu.VMEM
    dma = pltpu.SemaphoreType.DMA
    big = (slots, block, block)
    stripes = (n_t, block, tile)
    out = jax.ShapeDtypeStruct
    home, flat, left_new, right_new, first_new, second_new = pl.pallas_call(
        functools.partial(body, sizes),
        out_shape=(
            out((rows, shard_cols), BF16),
            out((rows_flat, cols), F32),
            out(big, F32), out(big, F32), out(big, F32), out(big, F32),
        ),
        in_specs=[SMEM, SMEM] + [ANY] * 8,
        out_specs=(ANY,) * 6,
        scratch_shapes=[
            vm((shard_tiles, block, tile), BF16),
            vm(stripes, BF16), vm(stripes, BF16), vm(stripes, BF16), vm(stripes, BF16),
            vm((slots * per_block, block, tile), BF16),
            vm((n_t * slots * per_block, rows_flat, tile), BF16),
            vm((rows, shard_cols), BF16), vm((rows_flat, cols), F32),
            vm((rows, shard_cols), F32),
            vm((n_t, rows_flat, shard_cols), jnp.int16), vm((n_t, rows_flat, shard_cols), jnp.int16),
            vm((n_t, 8, tile), F32), vm((n_t, 8, tile), F32),
            vm(big, F32), vm(big, F32), vm(big, BF16), vm(big, BF16), vm(big, BF16),
            vm(big, F32), vm(big, F32), vm(big, F32), vm(big, BF16),
            vm((8, tile), F32), vm((n_t, 8, tile), F32), vm((8, tile), F32), vm((n_dp, 8, tile), F32),
            pltpu.SMEM((slots * (per_block + 1),), jnp.int32),
            dma((7,)), dma((shard_tiles,)), dma((6,)),
            dma((n_t,)), dma((n_t,)), dma((n_t,)), dma((n_t,)), dma((n_t,)), dma((n_t,)), dma((n_t,)), dma((n_t,)),
            dma((slots, n_t)), dma((slots, n_t)),
            dma((n_t,)), dma((n_t,)), dma((n_dp,)), dma((n_dp,)), dma((3 + slots,)),
        ],
        compiler_params=pltpu.CompilerParams(
            collective_id=0, has_side_effects=True, vmem_limit_bytes=56 * 2**20
        ),
    )(
        block_owner, tile_block, gradient, fast_weight, left_stat, right_stat, left_basis, right_basis,
        first_moment, second_moment,
    )
    fast_new = fast_weight - STEP_RATE * home.astype(F32)
    slow_new = slow_flat + PULL_RATE * (flat - slow_flat)
    return (fast_new, slow_new, left_new, right_new, first_new, second_new)


def solution(mesh):
    square = P("dp", "tensor")
    spread = P(("dp", "tensor"), None)
    slot = P(("dp", "tensor"), None, None)
    return jax.shard_map(
        on_device,
        mesh=mesh,
        in_specs=(square, P(), P(), square, spread) + (slot,) * 6,
        out_specs=(square, spread) + (slot,) * 4,
        check_vma=False,
    )
```

```python
import functools

import jax
import jax.numpy as jnp
from jax import lax
from jax.experimental import pallas as pl
from jax.experimental.pallas import tpu as pltpu
from jax.sharding import PartitionSpec as P

BETA_STAT = 0.95
BETA_ONE = 0.9
BETA_TWO = 0.95
ADAM_EPS = 1e-08
STEP_RATE = 0.1
PULL_RATE = 0.5
CLIP_RMS = 0.5
F32 = jnp.float32
BF16 = jnp.bfloat16
ANY = pl.BlockSpec(memory_space=pl.ANY)
SMEM = pl.BlockSpec(memory_space=pltpu.SMEM)


def mm(a, b):
    return jnp.dot(a, b, preferred_element_type=F32)


def mm_nt(a, b):
    return lax.dot_general(a, b, (((1,), (1,)), ((), ())), preferred_element_type=F32)


def halves(x):
    high = x.astype(BF16)
    return high, (x - high.astype(F32)).astype(BF16)


def body(
    sizes,
    owner_ref, tiles_ref, grad_hbm, fast_hbm, left_hbm, right_hbm, lbase_hbm, rbase_hbm, first_hbm, second_hbm,
    fast_out, coded_out, scale_out, left_out, right_out, first_out, second_out,
    gt, pack, recv, back, returned, pieces, fast_v, coded, scale,
    left_v, right_v, lbase, rbase, lbase_t, first_v, second_v, pre, gblk,
    part, tens_sum, dp_part, dp_sum, table,
    in_sems, grad_sems, out_sems, g_send, g_recv, f_send, f_recv, c_send, c_recv, b_send, b_recv,
    s_send, s_recv, d_send, d_recv, own_sems,
):
    n_dp, n_t, slots, tile, shard_tiles, per_block, rows_flat, row_blocks, total = sizes
    t = lax.axis_index("tensor")
    dp = lax.axis_index("dp")

    def local(src, dst, sem):
        c = pltpu.make_async_copy(src, dst, sem)
        c.start()
        return c

    grad_in = [
        local(grad_hbm.at[:, pl.ds(i * tile, tile)], gt.at[i], grad_sems.at[i]) for i in range(shard_tiles)
    ]
    lb_in = local(lbase_hbm, lbase, in_sems.at[0])
    first_in = local(first_hbm, first_v, in_sems.at[1])
    rb_in = local(rbase_hbm, rbase, in_sems.at[2])
    second_in = local(second_hbm, second_v, in_sems.at[3])
    fast_in = local(fast_hbm, fast_v, in_sems.at[6])
    left_in = local(left_hbm, left_v, in_sems.at[4])
    right_in = local(right_hbm, right_v, in_sems.at[5])

    def to_t(d):
        return {"tensor": lax.rem(t + d, n_t)}

    def to_d(d):
        return {"dp": lax.rem(dp + d, n_dp)}

    barrier = pltpu.get_barrier_semaphore()
    for d in range(1, n_t):
        pl.semaphore_signal(barrier, inc=1, device_id=to_t(d), device_id_type=pl.DeviceIdType.MESH)
    for d in range(1, n_dp):
        pl.semaphore_signal(barrier, inc=1, device_id=to_d(d), device_id_type=pl.DeviceIdType.MESH)

    tb = [tiles_ref[dp, g] for g in range(n_t * shard_tiles)]
    my_owner = [
        lax.rem(owner_ref[tiles_ref[dp, t * shard_tiles + i]] // slots, n_t) for i in range(shard_tiles)
    ]
    send_tile = []
    for p in range(n_t):
        idx = jnp.int32(0)
        for i in range(shard_tiles):
            idx = jnp.where(my_owner[i] == p, i, idx)
        send_tile.append(idx)

    for c in grad_in:
        c.wait()

    def square(i, acc):
        wide = gt[i].astype(F32)
        return acc + jnp.sum((wide * wide).reshape(-1, 8, tile), axis=0)

    part[...] = lax.fori_loop(0, shard_tiles, square, jnp.zeros((8, tile), F32))
    for p in range(n_t):
        pack[p] = gt[send_tile[p]]
    pl.semaphore_wait(barrier, n_t + n_dp - 2)

    def remote(src, dst, ssem, rsem, to):
        return pltpu.make_async_remote_copy(
            src_ref=src, dst_ref=dst, send_sem=ssem, recv_sem=rsem, device_id=to,
            device_id_type=pl.DeviceIdType.MESH,
        )

    def peer(d):
        return lax.rem(t + d, n_t)

    def origin(d):
        return lax.rem(t + n_t - d, n_t)

    def sum_copy(d, slot):
        return remote(part, tens_sum.at[slot], s_send.at[d], s_recv.at[slot], to_t(d))

    def grad_copy(d, slot):
        return remote(pack.at[peer(d)], recv.at[slot], g_send.at[d], g_recv.at[slot], to_t(d))

    def code_copy(d, slot):
        return remote(coded.at[peer(d)], coded_out.at[slot], f_send.at[d], f_recv.at[slot], to_t(d))

    def scale_copy(d, slot):
        return remote(scale.at[peer(d)], scale_out.at[slot], c_send.at[d], c_recv.at[slot], to_t(d))

    def dp_copy(d, slot):
        return remote(dp_part, dp_sum.at[slot], d_send.at[d], d_recv.at[slot], to_d(d))

    def back_copy(d, slot):
        return remote(back.at[peer(d)], returned.at[slot], b_send.at[d], b_recv.at[slot], to_t(d))

    others = range(1, n_t)
    for d in others:
        sum_copy(d, t).start()
    for d in others:
        grad_copy(d, t).start()
    own_grad = local(pack.at[t], recv.at[t], own_sems.at[0])

    rank = []
    for a in range(n_t):
        count = jnp.int32(0)
        for b in range(a):
            same = tb[b * shard_tiles] == tb[a * shard_tiles]
            for i in range(1, shard_tiles):
                same = same | (tb[b * shard_tiles + i] == tb[a * shard_tiles])
            count = count + same.astype(jnp.int32)
        rank.append(count)
    present = []
    source = [jnp.int32(0)] * n_t
    for k in range(slots):
        block = jnp.int32(-1)
        slot_id = (dp * n_t + t) * slots + k
        for r in range(row_blocks):
            number = dp * row_blocks + r
            block = jnp.where(owner_ref[number] == slot_id, number, block)
        present.append(block >= 0)
        places = [jnp.int32(0)] * per_block
        for a in range(n_t):
            has = tb[a * shard_tiles] == block
            for i in range(1, shard_tiles):
                has = has | (tb[a * shard_tiles + i] == block)
            source[a] = jnp.where(has, k * per_block + rank[a], source[a])
            for j in range(per_block):
                places[j] = jnp.where(has & (rank[a] == j), a, places[j])
        for j in range(per_block):
            table[k * per_block + j] = places[j]
        table[slots * per_block + k] = (block >= 0).astype(jnp.int32)

    lb_in.wait()
    rb_in.wait()
    first_in.wait()

    def before(k, carry):
        turned = lbase[k].astype(F32).T.astype(BF16)
        lbase_t[k] = turned
        high, low = halves(first_v[k])
        high, low = halves(mm(turned, high) + mm(turned, low))
        pre[k] = BETA_ONE * (mm(high, rbase[k]) + mm(low, rbase[k]))
        return carry

    lax.fori_loop(0, slots, before, 0)

    for d in others:
        sum_copy(d, origin(d)).wait_recv()
    tens_sum[t] = part[...]
    dp_part[...] = jnp.sum(tens_sum[...], axis=0)
    for d in range(1, n_dp):
        dp_copy(d, dp).start()
    dp_sum[dp] = dp_part[...]
    for d in range(1, n_dp):
        dp_copy(d, lax.rem(dp + n_dp - d, n_dp)).wait_recv()
    square_sum = jnp.sum(jnp.sum(dp_sum[...], axis=0), axis=(0, 1), keepdims=True)
    factor = CLIP_RMS / jnp.sqrt(square_sum / total + 1e-06)

    for d in others:
        grad_copy(d, t).wait_send()
    own_grad.wait()
    for d in others:
        grad_copy(d, origin(d)).wait_recv()
    second_in.wait()

    def main(k, carry):
        for j in range(per_block):
            gblk[k, :, j * tile : (j + 1) * tile] = recv[table[k * per_block + j]]
        there = table[slots * per_block + k] > 0
        g = gblk[k]
        high, low = halves(mm(lbase_t[k], g))
        rotated = factor * (mm(high, rbase[k]) + mm(low, rbase[k]))
        fresh = BETA_TWO * second_v[k] + (1.0 - BETA_TWO) * rotated * rotated
        second_v[k] = jnp.where(there, fresh, second_v[k])
        direction = (pre[k] + (1.0 - BETA_ONE) * rotated) / (jnp.sqrt(fresh) + ADAM_EPS)
        high, low = halves(direction)
        high, low = halves(mm(lbase[k], high) + mm(lbase[k], low))
        update = (mm_nt(high, rbase[k]) + mm_nt(low, rbase[k])).astype(BF16)
        for j in range(per_block):
            pieces[k * per_block + j] = update[:, j * tile : (j + 1) * tile]
        return carry

    lax.fori_loop(0, slots, main, 0)
    for p in range(n_t):
        back[p] = pieces[source[p]]
    for d in others:
        back_copy(d, t).start()
    own_back = local(back.at[t], returned.at[t], own_sems.at[2])
    left_in.wait()
    right_in.wait()
    squared = (1.0 - BETA_STAT) * (factor * factor)

    def after(k, carry):
        there = table[slots * per_block + k] > 0
        g = gblk[k]
        wide = g.astype(F32)
        turned = wide.T.astype(BF16)
        left_v[k] = jnp.where(there, BETA_STAT * left_v[k] + squared * mm_nt(g, g), left_v[k])
        right_v[k] = jnp.where(there, BETA_STAT * right_v[k] + squared * mm(turned, g), right_v[k])
        first_v[k] = jnp.where(
            there, BETA_ONE * first_v[k] + ((1.0 - BETA_ONE) * factor) * wide, first_v[k]
        )
        return carry

    second_done = local(second_v, second_out, out_sems.at[0])
    lax.fori_loop(0, slots, after, 0)
    done = [
        second_done,
        local(left_v, left_out, out_sems.at[1]),
        local(right_v, right_out, out_sems.at[2]),
        local(first_v, first_out, out_sems.at[3]),
    ]

    fast_in.wait()
    own_back.wait()
    for d in others:
        back_copy(d, origin(d)).wait_recv()

    def encode(d):
        at = pl.ds(pl.multiple_of(peer(d) * rows_flat, rows_flat), rows_flat)
        for i in range(shard_tiles):
            lanes = slice(i * tile, (i + 1) * tile)
            fast_v[at, lanes] = fast_v[at, lanes] - STEP_RATE * returned[my_owner[i], at, :].astype(F32)
        x = fast_v[at, :]
        top = jnp.maximum(jnp.max(jnp.abs(x), axis=1, keepdims=True), 1e-30)
        coded[peer(d)] = jnp.floor(x * (32767.0 / top) + 0.5).astype(jnp.int32).astype(jnp.int16)
        wide = jnp.broadcast_to(top * (1.0 / 32767.0), (rows_flat, tile))
        scale[peer(d)] = jnp.concatenate([wide] * (tile // rows_flat), axis=0).T[:8]

    for d in others:
        encode(d)
        code_copy(d, t).start()
        scale_copy(d, t).start()
    encode(0)
    done += [
        local(coded.at[t], coded_out.at[t], own_sems.at[1]),
        local(scale.at[t], scale_out.at[t], own_sems.at[3]),
        local(fast_v, fast_out, out_sems.at[4]),
    ]
    for d in others:
        sum_copy(d, t).wait_send()
        back_copy(d, t).wait_send()
    for d in range(1, n_dp):
        dp_copy(d, dp).wait_send()
    for d in others:
        code_copy(d, t).wait_send()
        scale_copy(d, t).wait_send()
        code_copy(d, origin(d)).wait_recv()
        scale_copy(d, origin(d)).wait_recv()
    for c in done:
        c.wait()


def finish(coded_hbm, scale_hbm, slow_hbm, *refs):
    sources, slow_out, targets = refs[:5], refs[5], refs[6:11]
    coded, scale, slow = refs[11:14]
    held, in_sems, put_sems, sems = refs[14:19], refs[19], refs[20], refs[21]
    n_t, rows_flat, width = coded.shape
    tile = scale.shape[2]

    def local(src, dst, sem):
        c = pltpu.make_async_copy(src, dst, sem)
        c.start()
        return c

    first = [
        local(coded_hbm, coded, sems.at[0]),
        local(scale_hbm, scale, sems.at[1]),
        local(slow_hbm, slow, sems.at[2]),
    ]
    parts = [(n, h) for n in range(5) for h in range(2)]

    def half(ref, h):
        size = ref.shape[0] // 2
        return ref.at[pl.ds(h * size, size)]

    loads = [local(half(sources[n], h), half(held[n], h), in_sems.at[n, h]) for n, h in parts]
    for c in first:
        c.wait()
    puts = []
    for a in range(n_t):
        step = jnp.broadcast_to(scale[a, 0:1, :], (tile, tile)).T[:rows_flat]
        for i in range(width // tile):
            words = coded[a, :, i * tile : (i + 1) * tile].astype(jnp.int32)
            at = slice(a * width + i * tile, a * width + (i + 1) * tile)
            slow[:, at] = slow[:, at] + PULL_RATE * (words.astype(F32) * step - slow[:, at])
    puts.append(local(slow, slow_out, sems.at[3]))
    for (n, h), c in zip(parts, loads):
        c.wait()
        puts.append(local(half(held[n], h), half(targets[n], h), put_sems.at[n, h]))
    for c in puts:
        c.wait()


def on_device(
    gradient, block_owner, tile_block, fast_weight, slow_flat,
    left_stat, right_stat, left_basis, right_basis, first_moment, second_moment,
):
    block = left_stat.shape[1]
    slots = left_stat.shape[0]
    rows, shard_cols = gradient.shape
    n_t = lax.axis_size("tensor")
    n_dp = lax.axis_size("dp")
    tile_count = tile_block.shape[1]
    cols = shard_cols * n_t
    tile = cols // tile_count
    shard_tiles = shard_cols // tile
    per_block = block // tile
    rows_flat = block // n_t
    row_blocks = block_owner.shape[0] // n_dp
    sizes = (n_dp, n_t, slots, tile, shard_tiles, per_block, rows_flat, row_blocks, rows * cols * n_dp)
    vm = pltpu.VMEM
    dma = pltpu.SemaphoreType.DMA
    big = (slots, block, block)
    stripes = (n_t, block, tile)
    out = jax.ShapeDtypeStruct
    fast_new, coded, scale, left_new, right_new, first_new, second_new = pl.pallas_call(
        functools.partial(body, sizes),
        out_shape=(
            out((rows, shard_cols), F32),
            out((n_t, rows_flat, shard_cols), jnp.int16),
            out((n_t, 8, tile), F32),
            out(big, F32), out(big, F32), out(big, F32), out(big, F32),
        ),
        in_specs=[SMEM, SMEM] + [ANY] * 8,
        out_specs=(ANY,) * 7,
        scratch_shapes=[
            vm((shard_tiles, block, tile), BF16),
            vm(stripes, BF16), vm(stripes, BF16), vm(stripes, BF16), vm(stripes, BF16),
            vm((slots * per_block, block, tile), BF16),
            vm((rows, shard_cols), F32), vm((n_t, rows_flat, shard_cols), jnp.int16), vm((n_t, 8, tile), F32),
            vm(big, F32), vm(big, F32), vm(big, BF16), vm(big, BF16), vm(big, BF16),
            vm(big, F32), vm(big, F32), vm(big, F32), vm(big, BF16),
            vm((8, tile), F32), vm((n_t, 8, tile), F32), vm((8, tile), F32), vm((n_dp, 8, tile), F32),
            pltpu.SMEM((slots * (per_block + 1),), jnp.int32),
            dma((7,)), dma((shard_tiles,)), dma((6,)),
            dma((n_t,)), dma((n_t,)), dma((n_t,)), dma((n_t,)), dma((n_t,)), dma((n_t,)), dma((n_t,)), dma((n_t,)),
            dma((n_t,)), dma((n_t,)), dma((n_dp,)), dma((n_dp,)), dma((4,)),
        ],
        compiler_params=pltpu.CompilerParams(
            collective_id=0, has_side_effects=True, vmem_limit_bytes=56 * 2**20
        ),
    )(
        block_owner, tile_block, gradient, fast_weight, left_stat, right_stat, left_basis, right_basis,
        first_moment, second_moment,
    )
    states = (fast_new, left_new, right_new, first_new, second_new)
    slow_new, *states = pl.pallas_call(
        finish,
        out_shape=tuple(out(a.shape, F32) for a in (slow_flat,) + states),
        in_specs=[ANY] * 8,
        out_specs=(ANY,) * 6,
        scratch_shapes=[vm(coded.shape, jnp.int16), vm(scale.shape, F32), vm(slow_flat.shape, F32)]
        + [vm(a.shape, F32) for a in states]
        + [dma((5, 2)), dma((5, 2)), dma((4,))],
        compiler_params=pltpu.CompilerParams(vmem_limit_bytes=56 * 2**20),
    )(coded, scale, slow_flat, *states)
    fast_new, left_new, right_new, first_new, second_new = states
    return (fast_new, slow_new, left_new, right_new, first_new, second_new)


def solution(mesh):
    square = P("dp", "tensor")
    spread = P(("dp", "tensor"), None)
    slot = P(("dp", "tensor"), None, None)
    return jax.shard_map(
        on_device,
        mesh=mesh,
        in_specs=(square, P(), P(), square, spread) + (slot,) * 6,
        out_specs=(square, spread) + (slot,) * 4,
        check_vma=False,
    )
```
